256 devices in a mesh: acct: 64 (over x, z, core), rep: 4 (over y).
Axes of the slice: x: 4, y: 4, z: 8, core: 2. Of those that a mesh axis runs over, the one named last changes fastest.
Arguments:
- right_side: float32 [1048576, 64], P(('acct', 'rep')), may hold values from -6 to 6
- tile_account: int32 [16384, 128], P(('acct', 'rep')), may hold values from 0 to 127
- tile_attribute: int32 [16384, 128], P(('acct', 'rep')), may hold values from 0 to 127
- tile_count: int32 [16384], P(('acct', 'rep')), may hold values from 1 to 128
- tile_home: int32 [16384], P(('acct', 'rep')), may hold values from 0 to 31
- tile_block: int32 [16384], P(('acct', 'rep')), may hold values from 0 to 3
- attribute_weight: int32 [32768], P('acct'), may hold values from 1 to 4
Outputs:
- solution: float32 [1048576, 64], P(('acct', 'rep'))
- residual: float32 [1048576, 64], P(('acct', 'rep'))
The draws below stay inside these ranges and needn't reach their ends.
All inputs are finite; a program needn't handle non-finite values.
Results may differ from the reference program's by a relative error of at most 0.00035.
Values sent between devices are 32-bit elements; how exact they have to be, the bound alone decides.
No kernel may reach another device: no remote copies, remote signals or barrier semaphores. Data moves between devices by JAX's collectives and lax.ppermute only.
A program may use at most 64 MiB of HBM per device.

```python
import jax
import jax.numpy as jnp
from jax import lax

ACC_DEV = 4096
RHS = 64
TILE = 128
ATT_BLK = 4
SLOTS = 1
ITERS = 3
TILES_DEV = 64
ALL_TILES = 16384
ACCTS = 1048576
ATTRS = 32768
N_ACCT = 64
N_REP = 4


def touch_ends(result, key, least, top_value):
    longest = result.shape.index(max(result.shape))
    spots = []
    for shift in (0, 1):
        where = [jax.random.randint(jax.random.fold_in(key, axis), (), 0, length) for axis, length in enumerate(result.shape)]
        where[longest] = (where[longest] + shift) % result.shape[longest]
        spots.append(tuple(where))
    return result.at[spots[0]].set(least).at[spots[1]].set(top_value)


def steps_of(stream_key, shape, cuts, low, largest):
    gain, own = 1.0, jax.random.fold_in(stream_key, 6)
    for axis_at, shards_of in cuts:
        heights = jnp.exp(jax.random.uniform(jax.random.fold_in(own, axis_at), (shards_of,), jnp.float32, low / len(cuts), largest / len(cuts)))
        gain = gain * jnp.repeat(heights, shape[axis_at] // shards_of).reshape([-1 if axis == axis_at else 1 for axis in range(len(shape))])
    return gain


def bell_draw(rng, shape, width, reach, shards=(), kind=jnp.bfloat16):
    entries = jax.random.normal(rng, shape, jnp.float32) * width
    if len(shards) > 0:
        entries = steps_of(rng, shape, shards, -0.22, 0.18) * entries
    return jnp.clip(entries, min=-reach, max=reach).astype(kind)


def setup_inputs(seed: int = 0) -> dict:
    key_of = jax.random.split(jax.random.key(seed), 8)
    right_side = bell_draw(key_of[0], (ACCTS, RHS), 1.0, 6.0, ((0, 256),), jnp.float32)
    tile_account = touch_ends(jax.random.randint(key_of[1], (ALL_TILES, TILE), 0, TILE), jax.random.fold_in(key_of[1], 1), 0, TILE - 1).astype(jnp.int32)
    tile_attribute = touch_ends(jax.random.randint(key_of[2], (ALL_TILES, TILE), 0, TILE), jax.random.fold_in(key_of[2], 1), 0, TILE - 1).astype(jnp.int32)
    tile_count = touch_ends(jax.random.randint(key_of[3], (ALL_TILES,), 1, TILE + 1), jax.random.fold_in(key_of[3], 1), 1, TILE).astype(jnp.int32)
    tile_home = touch_ends(jax.random.randint(key_of[4], (ALL_TILES,), 0, ACC_DEV // TILE), jax.random.fold_in(key_of[4], 1), 0, (ACC_DEV // TILE) - 1).astype(jnp.int32)
    tile_block = touch_ends(jax.random.randint(key_of[5], (ALL_TILES,), 0, ATT_BLK), jax.random.fold_in(key_of[5], 1), 0, ATT_BLK - 1).astype(jnp.int32)
    attribute_weight = touch_ends(jax.random.randint(key_of[6], (ATTRS,), 1, 5), jax.random.fold_in(key_of[6], 1), 1, 4).astype(jnp.int32)
    return {"right_side": right_side, "tile_account": tile_account, "tile_attribute": tile_attribute, "tile_count": tile_count, "tile_home": tile_home, "tile_block": tile_block, "attribute_weight": attribute_weight}


def solve_spd(matrix, target):
    factor = jnp.linalg.cholesky(matrix)
    partway = lax.linalg.triangular_solve(factor, target, left_side=True, lower=True)
    return lax.linalg.triangular_solve(factor, partway, left_side=True, lower=True, transpose_a=True)

def inner_gram(first, second):
    return jnp.dot(first.T, second, precision=lax.Precision.HIGHEST)

def reference(right_side, tile_account, tile_attribute, tile_count, tile_home, tile_block, attribute_weight):
    sources = N_ACCT * N_REP
    slot_ids = jnp.arange(TILE, dtype=jnp.int32)
    tile_ids = jnp.arange(ALL_TILES, dtype=jnp.int32)
    source = tile_ids // TILES_DEV
    owner_dev = tile_ids % TILES_DEV // SLOTS
    account_index = (source * ACC_DEV + tile_home * TILE)[:, None] + tile_account
    attrib_index = (owner_dev * (ATT_BLK * TILE) + tile_block * TILE)[:, None] + tile_attribute
    usable = (slot_ids[None, :] < tile_count[:, None]).astype(jnp.float32)
    weight = attribute_weight.astype(jnp.float32)
    flat_acc = account_index.reshape(-1)
    flat_att = attrib_index.reshape(-1)
    flat_use = usable.reshape(-1)
    counts = jnp.zeros((ATTRS,), jnp.float32).at[flat_att].add(flat_use)
    weighted = counts * weight
    degree = jnp.zeros((ACCTS,), jnp.float32).at[flat_acc].add(flat_use * weighted[flat_att])
    acc_rows = account_index.reshape(sources, TILES_DEV * TILE)
    att_rows = attrib_index.reshape(sources, TILES_DEV * TILE)
    use_rows = usable.reshape(sources, TILES_DEV * TILE)

    def couple(vector):

        def gather_step(running, pieces):
            account, attrib, valid = pieces
            return (running.at[attrib].add(valid[:, None] * vector[account]), None)
        attr_sums, unused = lax.scan(gather_step, jnp.zeros((ATTRS, RHS), jnp.float32), (acc_rows, att_rows, use_rows))
        scaled = attr_sums * weight[:, None]

        def spread_step(running, pieces):
            account, attrib, valid = pieces
            return (running.at[account].add(valid[:, None] * scaled[attrib]), None)
        linked_entries, unused = lax.scan(spread_step, jnp.zeros((ACCTS, RHS), jnp.float32), (acc_rows, att_rows, use_rows))
        return vector + 0.0625 * (degree[:, None] * vector - linked_entries)
    solution = jnp.zeros((ACCTS, RHS), jnp.float32)
    residual = right_side
    direction = right_side
    res_gram = inner_gram(residual, residual)
    for iteration in range(ITERS):
        product = couple(direction)
        curvature = inner_gram(direction, product)
        step_size = solve_spd(curvature, res_gram)
        solution = solution + jnp.dot(direction, step_size, precision=lax.Precision.HIGHEST)
        residual = residual - jnp.dot(product, step_size, precision=lax.Precision.HIGHEST)
        if iteration + 1 < ITERS:
            new_gram = inner_gram(residual, residual)
            update = solve_spd(res_gram, new_gram)
            direction = residual + jnp.dot(direction, update, precision=lax.Precision.HIGHEST)
            res_gram = new_gram
    return (solution, residual)
```

```python
import jax
import jax.numpy as jnp
from jax import lax
from jax.experimental import pallas as pl
from jax.experimental.pallas import tpu as pltpu
from jax.sharding import Mesh, PartitionSpec as P

ITERS = 3
NX, NZ, NC, NY = 4, 8, 2, 4
TILE = 128
COLS = 64
BLOCKS = 4
HALF = NZ // 2
COUPLING = 0.0625
ALL = ("x", "z", "core", "rep")
VMEM = pl.BlockSpec(memory_space=pltpu.VMEM)
SMEM = pl.BlockSpec(memory_space=pltpu.SMEM)
NT = (((1,), (1,)), ((), ()))
PARAMS = pltpu.CompilerParams(vmem_limit_bytes=40 * 1024 * 1024)


def shape(*dims, dtype=jnp.float32):
    return jax.ShapeDtypeStruct(dims, dtype)


def solve_spd(matrix, target):
    factor = jnp.linalg.cholesky(matrix)
    partway = lax.linalg.triangular_solve(factor, target, left_side=True, lower=True)
    return lax.linalg.triangular_solve(
        factor, partway, left_side=True, lower=True, transpose_a=True
    )


def mul(first, second):
    return jnp.dot(first, second, precision=lax.Precision.HIGHEST)


def gram(first, second):
    return lax.dot_general(first, second, NT, precision=lax.Precision.HIGHEST)


def shift(value, axis, size, distance):
    return lax.ppermute(value, axis, [(i, (i + distance) % size) for i in range(size)])


def swap(value):
    return lax.ppermute(value, "core", [(0, 1), (1, 0)])


def sum_all(value):
    for axis, size in (("core", NC), ("x", NX), ("rep", NY), ("z", NZ)):
        step = 1
        while step < size:
            value = value + lax.ppermute(value, axis, [(i, i ^ step) for i in range(size)])
            step *= 2
    return value


def tile_order():
    return [
        (half, step, core, spot)
        for half in range(2)
        for step in range(4)
        for core in range(2)
        for spot in range(HALF)
    ]


def tile_number(place, half, step, spot):
    x_at, core_at, y_at = place
    x_owner = lax.rem((y_at if half == 0 else x_at) + step, NX)
    return (x_owner * NZ + half * HALF + spot) * NC + core_at


def build_kernel(place_ref, count_ref, acct_ref, attr_ref, tiles_ref, turned_ref, sums_ref):
    place = place_ref[0], place_ref[1], place_ref[2]
    rows = lax.broadcasted_iota(jnp.int32, (TILE, TILE), 0)
    lanes = lax.broadcasted_iota(jnp.int32, (TILE, TILE), 1)
    for n, (half, step, core, spot) in enumerate(tile_order()):
        t = tile_number(place, half, step, spot)
        account = acct_ref[core, pl.ds(t, 1), :]
        attrib = attr_ref[core, pl.ds(t, 1), :]
        used = lanes < count_ref[core, t]
        account_hot = jnp.where((rows == account) & used, 1.0, 0.0).astype(jnp.bfloat16)
        attrib_hot = jnp.where(rows == attrib, 1.0, 0.0).astype(jnp.bfloat16)
        tile = lax.dot_general(
            account_hot, attrib_hot, NT, preferred_element_type=jnp.float32
        )
        turned = lax.dot_general(
            attrib_hot, account_hot, NT, preferred_element_type=jnp.float32
        )
        tiles_ref[n] = tile.astype(jnp.bfloat16)
        turned_ref[n] = turned.astype(jnp.bfloat16)
        sums_ref[pl.ds(n, 1), :] = jnp.sum(tile, axis=0, keepdims=True)


def build(place, counts, accounts, attribs):
    return pl.pallas_call(
        build_kernel,
        out_shape=(
            shape(64, TILE, TILE, dtype=jnp.bfloat16),
            shape(64, TILE, TILE, dtype=jnp.bfloat16),
            shape(64, TILE),
        ),
        in_specs=[SMEM, SMEM, VMEM, VMEM],
        out_specs=(VMEM, VMEM, VMEM),
        compiler_params=PARAMS,
        name="build_tiles",
    )(place, counts, accounts, attribs)


def pieces(value):
    high = value.astype(jnp.bfloat16)
    rest = value - high.astype(jnp.float32)
    middle = rest.astype(jnp.bfloat16)
    low = (rest - middle.astype(jnp.float32)).astype(jnp.bfloat16)
    return high, middle, low


def gather_kernel(place_ref, home_ref, own_ref, sib_ref, tiles_ref, *refs):
    sums_ref = refs[0] if len(refs) == 10 else None
    outs, split = refs[-9:-1], refs[-1]
    place = place_ref[0], place_ref[1], place_ref[2]
    for core, ref in enumerate((own_ref, sib_ref)):
        for part, piece in enumerate(pieces(ref[...])):
            split[core, part * COLS : (part + 1) * COLS, :] = piece
    for n, (half, step, core, spot) in enumerate(tile_order()):
        home = home_ref[core, tile_number(place, half, step, spot)]
        block = split[core, :, pl.ds(pl.multiple_of(home * TILE, TILE), TILE)]
        parts = jnp.dot(block, tiles_ref[n], preferred_element_type=jnp.float32)
        out = outs[half * 4 + step]
        at = core * HALF + spot
        out[at, :COLS, :] = parts[:COLS] + (parts[COLS : 2 * COLS] + parts[2 * COLS :])
        if sums_ref is not None:
            out[at, COLS:, :] = jnp.broadcast_to(sums_ref[pl.ds(n, 1), :], (8, TILE))


def gather(place, homes, own, sib, tiles, sums):
    rows = COLS if sums is None else COLS + 8
    extra = () if sums is None else (sums,)
    return pl.pallas_call(
        gather_kernel,
        out_shape=tuple(shape(2 * HALF, rows, TILE) for _ in range(8)),
        in_specs=[SMEM, SMEM, VMEM, VMEM, VMEM] + [VMEM] * len(extra),
        out_specs=tuple(VMEM for _ in range(8)),
        scratch_shapes=[pltpu.VMEM((2, 3 * COLS, own.shape[1]), jnp.bfloat16)],
        compiler_params=PARAMS,
        name="gather_tiles",
    )(place, homes, own, sib, tiles, *extra)


def collect_kernel(place_ref, blocks_ref, *refs):
    ins, outs, total = refs[:8], refs[8:16], refs[16]
    for half in range(2):
        mine = place_ref[0] if half == 0 else place_ref[2]
        total[...] = jnp.zeros_like(total)
        for step in range(4):
            for core in range(2):
                for spot in range(HALF):
                    at = core * HALF + spot
                    block = blocks_ref[half * 4 + step, at]
                    slot = lax.rem(block - mine + BLOCKS, BLOCKS)
                    total[slot, spot] += ins[half * 4 + step][at]
        for step in range(4):
            outs[half * 4 + step][...] = total[step]


def collect(place, blocks, arrays):
    rows = arrays[0].shape[1]
    return pl.pallas_call(
        collect_kernel,
        out_shape=tuple(shape(HALF, rows, TILE) for _ in range(8)),
        in_specs=[SMEM, SMEM] + [VMEM] * 8,
        out_specs=tuple(VMEM for _ in range(8)),
        scratch_shapes=[pltpu.VMEM((BLOCKS, HALF, rows, TILE), jnp.float32)],
        compiler_params=PARAMS,
        name="collect_blocks",
    )(place, blocks, *arrays)


def expand_kernel(place_ref, blocks_ref, *refs):
    ins, outs, table = refs[:8], refs[8:16], refs[16]
    for half in range(2):
        mine = place_ref[0] if half == 0 else place_ref[2]
        for step in range(4):
            table[step] = ins[half * 4 + step][...]
        for step in range(4):
            for core in range(2):
                for spot in range(HALF):
                    at = core * HALF + spot
                    block = blocks_ref[half * 4 + step, at]
                    slot = lax.rem(mine - block + BLOCKS, BLOCKS)
                    outs[half * 4 + step][at] = table[slot, spot]


def expand(place, blocks, arrays):
    rows = arrays[0].shape[1]
    return pl.pallas_call(
        expand_kernel,
        out_shape=tuple(shape(2 * HALF, rows, TILE) for _ in range(8)),
        in_specs=[SMEM, SMEM] + [VMEM] * 8,
        out_specs=tuple(VMEM for _ in range(8)),
        scratch_shapes=[pltpu.VMEM((BLOCKS, HALF, rows, TILE), jnp.float32)],
        compiler_params=PARAMS,
        name="expand_blocks",
    )(place, blocks, *arrays)


def spread_kernel(place_ref, home_ref, turned_ref, *refs):
    ins, outs = refs[:8], refs[8:10]
    place = place_ref[0], place_ref[1], place_ref[2]
    for out in outs:
        out[...] = jnp.zeros_like(out)
    rows = outs[0].shape[0]
    for n, (half, step, core, spot) in enumerate(tile_order()):
        home = home_ref[core, tile_number(place, half, step, spot)]
        value = ins[half * 4 + step][core * HALF + spot]
        stack = jnp.concatenate([p.astype(jnp.float32) for p in pieces(value)], axis=0)
        parts = jnp.dot(
            stack.astype(jnp.bfloat16), turned_ref[n], preferred_element_type=jnp.float32
        )
        where = pl.ds(pl.multiple_of(home * TILE, TILE), TILE)
        outs[core][:, where] += parts[:rows] + (parts[rows : 2 * rows] + parts[2 * rows :])


def spread(place, homes, turned, arrays, accounts):
    rows = arrays[0].shape[1]
    return pl.pallas_call(
        spread_kernel,
        out_shape=(shape(rows, accounts), shape(rows, accounts)),
        in_specs=[SMEM, SMEM, VMEM] + [VMEM] * 8,
        out_specs=(VMEM, VMEM),
        compiler_params=PARAMS,
        name="spread_tiles",
    )(place, homes, turned, *arrays)


def send_halves(arrays, near, far, sign):
    got = []
    for half, axis in ((0, near), (1, far)):
        size = NY if axis == "rep" else NX
        got.append(arrays[half * 4])
        for step in range(1, 4):
            got.append(shift(arrays[half * 4 + step], axis, size, sign * step))
    return got


def couple(place, homes, blocks, tiles, turned, weight, own, sib, sums):
    messages = gather(place, homes, own, sib, tiles, sums)
    arrived = send_halves(messages, "rep", "x", 1)
    dense = collect(place, blocks, arrived)
    arrived = send_halves(dense, "x", "rep", 1)
    halves = [
        (arrived[h] + arrived[h + 1]) + (arrived[h + 2] + arrived[h + 3]) for h in (0, 4)
    ]
    parts = lax.all_to_all(
        jnp.concatenate(halves, axis=0), "z", split_axis=0, concat_axis=0, tiled=True
    )
    scaled = jnp.sum(parts, axis=0) * weight
    values = lax.all_to_all(
        jnp.broadcast_to(scaled, parts.shape), "z", split_axis=0, concat_axis=0, tiled=True
    )
    arrived = send_halves(
        [values[:HALF]] * 4 + [values[HALF:]] * 4, "x", "rep", 1
    )
    entries = expand(place, blocks, arrived)
    arrived = send_halves(entries, "rep", "x", -1)
    mine, other = spread(place, homes, turned, arrived, own.shape[1])
    return mine + swap(other)


def shards(
    right_side, tile_account, tile_attribute, tile_count, tile_home, tile_block, attribute_weight
):
    x_at, z_at = lax.axis_index("x"), lax.axis_index("z")
    core_at, y_at = lax.axis_index("core"), lax.axis_index("rep")
    place = jnp.stack([x_at, core_at, y_at])
    start = right_side.T

    info = jnp.concatenate(
        [
            tile_account,
            tile_attribute,
            jnp.pad(jnp.stack([tile_count, tile_home, tile_block]), ((0, 5), (0, 64))),
        ],
        axis=0,
    )
    info = jnp.stack([info, swap(info)])
    accounts, attribs = info[:, :64], info[:, 64:128]
    counts, homes, tile_blocks = info[:, 128, :64], info[:, 129, :64], info[:, 130, :64]
    by_owner = lax.dynamic_index_in_dim(
        tile_blocks.reshape(2, NX, 2, HALF, NC), core_at, 4, keepdims=False
    )
    blocks = []
    for half, axis, at in ((0, "rep", y_at), (1, "x", x_at)):
        for step in range(4):
            ids = lax.dynamic_index_in_dim(
                by_owner[:, :, half], lax.rem(at + step, NX), 1, keepdims=False
            ).reshape(2 * HALF)
            blocks.append(ids if step == 0 else shift(ids, axis, 4, step))
    blocks = jnp.stack(blocks)

    own_weight = attribute_weight.reshape(BLOCKS, TILE)
    all_weight = lax.all_gather(own_weight, "x", axis=0, tiled=False)
    first = lax.dynamic_index_in_dim(
        lax.dynamic_index_in_dim(all_weight, y_at, 0, keepdims=False), x_at, 0, keepdims=False
    )
    second = lax.dynamic_index_in_dim(own_weight, y_at, 0, keepdims=False)
    weight = jnp.where(z_at < HALF, first, second).astype(jnp.float32)[None, :]

    tiles, turned, sums = build(place, counts, accounts, attribs)

    def link(vector, with_sums):
        return couple(
            place,
            homes,
            blocks,
            tiles,
            turned,
            weight,
            vector,
            swap(vector),
            sums if with_sums else None,
        )

    linked = link(start, True)
    degree = linked[COLS : COLS + 1]
    product = start + COUPLING * (degree * start - linked[:COLS])

    def operate(vector):
        return vector + COUPLING * (degree * vector - link(vector, False))

    grams = sum_all(
        jnp.concatenate([gram(start, start), gram(start, product), gram(product, product)])
    )
    res_gram, curvature, square = grams[:COLS], grams[COLS : 2 * COLS], grams[2 * COLS :]
    step_0 = solve_spd(curvature, res_gram)
    cross = mul(curvature, step_0)
    next_gram = res_gram - cross - cross.T + mul(step_0.T, mul(square, step_0))
    update_0 = solve_spd(res_gram, next_gram)
    twice = operate(product)

    residual = start - mul(step_0.T, product)
    direction = residual + mul(update_0.T, start)
    image = product - mul(step_0.T, twice)
    product_1 = image + mul(update_0.T, product)

    grams = sum_all(
        jnp.concatenate(
            [
                gram(residual, residual),
                gram(direction, product_1),
                gram(residual, product_1),
                gram(product_1, product_1),
            ]
        )
    )
    res_gram, curvature, mixed, square = (grams[i * COLS : (i + 1) * COLS] for i in range(4))
    step_1 = solve_spd(curvature, res_gram)
    cross = mul(mixed, step_1)
    next_gram = res_gram - cross - cross.T + mul(step_1.T, mul(square, step_1))
    update_1 = solve_spd(res_gram, next_gram)
    twice = operate(product_1)

    solution_2 = mul(step_0.T, start) + mul(step_1.T, direction)
    residual = residual - mul(step_1.T, product_1)
    direction = residual + mul(update_1.T, direction)
    product_2 = image - mul(step_1.T, twice) + mul(update_1.T, product_1)

    grams = sum_all(
        jnp.concatenate([gram(residual, residual), gram(direction, product_2)])
    )
    step_2 = solve_spd(grams[COLS:], grams[:COLS])
    answer = solution_2 + mul(step_2.T, direction)
    residual = residual - mul(step_2.T, product_2)
    return (answer.T, residual.T)


def solution(mesh):
    fine = Mesh(mesh.devices.reshape(NX, NZ, NC, NY), ALL)
    rows, flat = P(ALL, None), P(ALL)
    return jax.shard_map(
        shards,
        mesh=fine,
        in_specs=(rows, rows, rows, flat, flat, flat, P(("x", "z", "core"))),
        out_specs=(rows, rows),
        check_vma=False,
    )
```

```python
import jax
import jax.numpy as jnp
from jax import lax
from jax.experimental import pallas as pl
from jax.experimental.pallas import tpu as pltpu
from jax.sharding import Mesh, PartitionSpec as P

NX, NZ, NC, NY = 4, 8, 2, 4
TILE = 128
COLS = 64
BLOCKS = 4
TILES = 64
PART = COLS // NY
BODY = NZ * PART
EXTRA = 8
PEERS = NX * NC * NY
COUPLING = 0.0625
ALL = ("x", "z", "core", "rep")
NEAR = ("x", "core", "rep")
SIZES = {"x": NX, "z": NZ, "core": NC, "rep": NY}
VMEM = pl.BlockSpec(memory_space=pltpu.VMEM)
SMEM = pl.BlockSpec(memory_space=pltpu.SMEM)
NT = (((1,), (1,)), ((), ()))
TN = (((0,), (0,)), ((), ()))
PARAMS = pltpu.CompilerParams(vmem_limit_bytes=40 * 1024 * 1024)


def shape(*dims, dtype=jnp.float32):
    return jax.ShapeDtypeStruct(dims, dtype)


def mul(first, second):
    return jnp.dot(first, second, precision=lax.Precision.HIGHEST)


def turn_mul(first, second):
    return lax.dot_general(first, second, TN, precision=lax.Precision.HIGHEST)


def gram(first, second):
    return lax.dot_general(first, second, NT, precision=lax.Precision.HIGHEST)


def swap_parts(value, axes):
    return lax.all_to_all(value, axes, split_axis=0, concat_axis=0, tiled=True)


def sum_over(value, *axes):
    for axis in axes:
        size, step = SIZES[axis], 1
        while step < size:
            value = value + lax.ppermute(value, axis, [(i, i ^ step) for i in range(size)])
            step *= 2
    return value


def tile_places():
    return [
        (t, (t // (NZ * NC) * NC + t % NC) * NY, t // NC % NZ) for t in range(TILES)
    ]


def pieces(value):
    high = value.astype(jnp.bfloat16)
    rest = value - high.astype(jnp.float32)
    middle = rest.astype(jnp.bfloat16)
    low = (rest - middle.astype(jnp.float32)).astype(jnp.bfloat16)
    return high, middle, low


def build_kernel(count_ref, acct_ref, attr_ref, tiles_ref, turned_ref, sums_ref):
    rows = lax.broadcasted_iota(jnp.int32, (TILE, TILE), 0)
    lanes = lax.broadcasted_iota(jnp.int32, (TILE, TILE), 1)
    for t in range(TILES):
        used = lanes < count_ref[t]
        account_hot = jnp.where((rows == acct_ref[t : t + 1, :]) & used, 1.0, 0.0)
        attrib_hot = jnp.where(rows == attr_ref[t : t + 1, :], 1.0, 0.0)
        account_hot = account_hot.astype(jnp.bfloat16)
        attrib_hot = attrib_hot.astype(jnp.bfloat16)
        tile = lax.dot_general(
            account_hot, attrib_hot, NT, preferred_element_type=jnp.float32
        )
        turned = lax.dot_general(
            attrib_hot, account_hot, NT, preferred_element_type=jnp.float32
        )
        tiles_ref[t] = tile.astype(jnp.bfloat16)
        turned_ref[t] = turned.astype(jnp.bfloat16)
        sums_ref[t : t + 1, :] = jnp.sum(tile, axis=0, keepdims=True)


def build(counts, accounts, attribs):
    return pl.pallas_call(
        build_kernel,
        out_shape=(
            shape(TILES, TILE, TILE, dtype=jnp.bfloat16),
            shape(TILES, TILE, TILE, dtype=jnp.bfloat16),
            shape(TILES, TILE),
        ),
        in_specs=[SMEM, VMEM, VMEM],
        out_specs=(VMEM, VMEM, VMEM),
        compiler_params=PARAMS,
        name="build_tiles",
    )(counts, accounts, attribs)


def gather_kernel(first, home_ref, vector_ref, tiles_ref, *refs):
    out, split = refs[-2:]
    for part, piece in enumerate(pieces(vector_ref[...])):
        split[part * COLS : (part + 1) * COLS, :] = piece
    if first:
        extra_ref, ids = refs[:2]
        for m in range(PEERS):
            out[m, BODY + 2 :, :] = jnp.broadcast_to(ids[m : m + 1, :], (EXTRA - 2, TILE))
    for t, m, z in tile_places():
        home = home_ref[t]
        block = split[:, pl.ds(pl.multiple_of(home * TILE, TILE), TILE)]
        parts = jnp.dot(block, tiles_ref[t], preferred_element_type=jnp.float32)
        value = parts[:COLS] + (parts[COLS : 2 * COLS] + parts[2 * COLS :])
        for y in range(NY):
            out[m + y, z * PART : (z + 1) * PART, :] = value[y * PART : (y + 1) * PART]
        if first:
            row = BODY + z % 2
            out[m + z // 2, row : row + 1, :] = extra_ref[t : t + 1, :]


def gather(homes, vector, tiles, *extras):
    return pl.pallas_call(
        lambda *refs: gather_kernel(len(extras) > 0, *refs),
        out_shape=shape(PEERS, BODY + (EXTRA if extras else 0), TILE),
        in_specs=[SMEM] + [VMEM] * (2 + len(extras)),
        out_specs=VMEM,
        scratch_shapes=[pltpu.VMEM((3 * COLS, vector.shape[1]), jnp.bfloat16)],
        compiler_params=PARAMS,
        name="gather_tiles",
    )(homes, vector, tiles, *extras)


def collect_kernel(first, place_ref, blocks_ref, in_ref, out_ref):
    out_ref[...] = jnp.zeros_like(out_ref)
    for m in range(PEERS):
        for z in range(NZ):
            at = pl.ds(pl.multiple_of(blocks_ref[m, z] * PART, PART), PART)
            out_ref[z, at, :] += in_ref[m, z * PART : (z + 1) * PART, :]
    if first:
        for m in range(PEERS):
            for i in range(2):
                z = place_ref[0] * 2 + i
                at = pl.ds(COLS + blocks_ref[m, z], 1)
                out_ref[z, at, :] += in_ref[m, BODY + i : BODY + i + 1, :]


def collect(first, place, blocks, arrived):
    return pl.pallas_call(
        lambda *refs: collect_kernel(first, *refs),
        out_shape=shape(NZ, COLS + (EXTRA if first else 0), TILE),
        in_specs=[SMEM, SMEM, VMEM],
        out_specs=VMEM,
        compiler_params=PARAMS,
        name="collect_blocks",
    )(place, blocks, arrived)


def scale_kernel(first, in_ref, weight_ref, out_ref, sums_ref):
    total = in_ref[0]
    for z in range(1, NZ):
        total = total + in_ref[z]
    weight = weight_ref[...].astype(jnp.float32)
    scaled = [
        total[b * PART : (b + 1) * PART] * weight[b : b + 1] for b in range(BLOCKS)
    ]
    sums_ref[...] = total[:COLS]
    for z in range(NZ):
        for b in range(BLOCKS):
            out_ref[z, b * PART : (b + 1) * PART, :] = scaled[b]
        if first:
            out_ref[z, COLS : COLS + BLOCKS, :] = total[COLS : COLS + BLOCKS] * weight
            out_ref[z, COLS + BLOCKS :, :] = total[COLS + BLOCKS :]


def scale(first, parts, weight):
    return pl.pallas_call(
        lambda *refs: scale_kernel(first, *refs),
        out_shape=(shape(NZ, COLS + (EXTRA if first else 0), TILE), shape(COLS, TILE)),
        in_specs=[VMEM, VMEM],
        out_specs=(VMEM, VMEM),
        compiler_params=PARAMS,
        name="scale_sums",
    )(parts, weight)


def expand_kernel(first, place_ref, blocks_ref, in_ref, out_ref):
    for m in range(PEERS):
        for z in range(NZ):
            at = pl.ds(pl.multiple_of(blocks_ref[m, z] * PART, PART), PART)
            out_ref[m, z * PART : (z + 1) * PART, :] = in_ref[z, at, :]
        if first:
            out_ref[m, BODY:, :] = jnp.zeros((EXTRA, TILE), jnp.float32)
            for i in range(2):
                z = place_ref[0] * 2 + i
                at = pl.ds(COLS + blocks_ref[m, z], 1)
                out_ref[m, BODY + i : BODY + i + 1, :] = in_ref[z, at, :]


def expand(first, place, blocks, values):
    return pl.pallas_call(
        lambda *refs: expand_kernel(first, *refs),
        out_shape=shape(PEERS, BODY + (EXTRA if first else 0), TILE),
        in_specs=[SMEM, SMEM, VMEM],
        out_specs=VMEM,
        compiler_params=PARAMS,
        name="expand_blocks",
    )(place, blocks, values)


def spread_kernel(first, home_ref, turned_ref, in_ref, out_ref):
    out_ref[...] = jnp.zeros_like(out_ref)
    rows = out_ref.shape[0]
    for t, m, z in tile_places():
        at = pl.ds(pl.multiple_of(home_ref[t] * TILE, TILE), TILE)
        values = [in_ref[m + y, z * PART : (z + 1) * PART, :] for y in range(NY)]
        if first:
            row = BODY + z % 2
            count = in_ref[m + z // 2, row : row + 1, :]
            values.append(jnp.broadcast_to(count, (EXTRA, TILE)))
        split = pieces(jnp.concatenate(values, axis=0))
        stack = jnp.concatenate([p.astype(jnp.float32) for p in split], axis=0)
        parts = jnp.dot(
            stack.astype(jnp.bfloat16), turned_ref[t], preferred_element_type=jnp.float32
        )
        out_ref[:, at] += parts[:rows] + (parts[rows : 2 * rows] + parts[2 * rows :])


def spread(first, homes, turned, arrived, accounts):
    rows = COLS + (EXTRA if first else 0)
    return pl.pallas_call(
        lambda *refs: spread_kernel(first, *refs),
        out_shape=shape(rows, accounts),
        in_specs=[SMEM, VMEM, VMEM],
        out_specs=VMEM,
        compiler_params=PARAMS,
        name="spread_tiles",
    )(homes, turned, arrived)


def eliminate(systems):
    rows = lax.broadcasted_iota(jnp.int32, (COLS, 2 * COLS), 0)
    for k in range(COLS):
        after = []
        for system in systems:
            pivot = system[k : k + 1, :] * (1.0 / system[k : k + 1, k : k + 1])
            rest = system - system[:, k : k + 1] * pivot
            after.append(jnp.where(rows == k, pivot, rest))
        systems = after
    return [system[:, COLS:] for system in systems]


def step_kernel(pack_ref, step_ref, update_ref, next_ref):
    res_gram = pack_ref[:, COLS : 2 * COLS]
    mixed, square = pack_ref[:, 2 * COLS : 3 * COLS], pack_ref[:, 3 * COLS : 4 * COLS]
    rows = lax.broadcasted_iota(jnp.int32, (COLS, COLS), 0)
    unit = (rows == lax.broadcasted_iota(jnp.int32, (COLS, COLS), 1)).astype(jnp.float32)
    step, inverse = eliminate(
        [pack_ref[:, : 2 * COLS], jnp.concatenate([res_gram, unit], axis=1)]
    )
    cross = mul(mixed, step)
    next_gram = res_gram - cross - cross.T + turn_mul(step, mul(square, step))
    step_ref[...] = step
    update_ref[...] = mul(inverse, next_gram)
    next_ref[...] = next_gram


def steps(pack):
    return pl.pallas_call(
        step_kernel,
        out_shape=(shape(COLS, COLS),) * 3,
        in_specs=[VMEM],
        out_specs=(VMEM,) * 3,
        compiler_params=PARAMS,
        name="step_matrices",
    )(pack)


def owner_gram_kernel(place_ref, in_ref, weight_ref, out_ref, whole):
    weight = weight_ref[...].astype(jnp.float32)
    for d in range(NY):
        source = lax.rem(place_ref[0] + NY - d, NY)
        at = pl.ds(pl.multiple_of(source * PART, PART), PART)
        for b in range(BLOCKS):
            whole[at, b * TILE : (b + 1) * TILE] = in_ref[d, b * PART : (b + 1) * PART, :]
    scale = jnp.concatenate([weight[b : b + 1] for b in range(BLOCKS)], axis=1)
    out_ref[...] = gram(whole[...] * scale, whole[...])


def owner_gram(place, quarters, weight):
    return pl.pallas_call(
        owner_gram_kernel,
        out_shape=shape(COLS, COLS),
        in_specs=[SMEM, VMEM, VMEM],
        out_specs=VMEM,
        scratch_shapes=[pltpu.VMEM((COLS, BLOCKS * TILE), jnp.float32)],
        compiler_params=PARAMS,
        name="owner_gram",
    )(place, quarters, weight)


def last_kernel(pack_ref, linked_ref, step_ref, update_ref, next_ref, last_ref):
    curvature = pack_ref[:, :COLS]
    mixed, square = pack_ref[:, 2 * COLS : 3 * COLS], pack_ref[:, 3 * COLS : 4 * COLS]
    image_r, image_p = pack_ref[:, 4 * COLS : 5 * COLS], pack_ref[:, 5 * COLS : 6 * COLS]
    step, update = step_ref[...], update_ref[...]
    own = pack_ref[:, 6 * COLS : 7 * COLS] - COUPLING * linked_ref[...]
    half = mul(mixed, update) - mul(image_p, step) - turn_mul(step, mul(square, update))
    whole = image_r + turn_mul(step, mul(own, step))
    whole = whole + turn_mul(update, mul(curvature, update)) + half + half.T
    last_ref[...] = eliminate([jnp.concatenate([whole, next_ref[...]], axis=1)])[0]


def last_step(*matrices):
    return pl.pallas_call(
        last_kernel,
        out_shape=shape(COLS, COLS),
        in_specs=[VMEM] * 5,
        out_specs=VMEM,
        compiler_params=PARAMS,
        name="last_step_matrix",
    )(*matrices)


def shards(
    right_side, tile_account, tile_attribute, tile_count, tile_home, tile_block, attribute_weight
):
    y_at = lax.axis_index("rep")
    place = y_at.reshape(1)
    start = right_side.T
    weight = attribute_weight.reshape(BLOCKS, TILE)
    tiles, turned, sums = build(tile_count, tile_account, tile_attribute)
    ids = tile_block.reshape(NX, NZ, NC).transpose(0, 2, 1).reshape(NX * NC, NZ)
    ids = jnp.pad(
        jnp.repeat(ids, NY, axis=0).astype(jnp.float32), ((0, 0), (0, TILE - NZ))
    )

    def finish(first, blocks, arrived, grams, last=False):
        if grams is not None:
            grams = sum_over(grams, "z")
            arrived, grams = lax.optimization_barrier((arrived, grams))
            grams = sum_over(grams, "core", "x")
        parts = swap_parts(collect(first, place, blocks, arrived), "z")
        if grams is not None:
            parts, grams = lax.optimization_barrier((parts, grams))
            grams = sum_over(grams, "rep")
        values, totals = scale(first, parts, weight)
        values = swap_parts(values, "z")
        if last:
            totals = [totals] + [
                lax.ppermute(totals, "rep", [(i, (i + d) % NY) for i in range(NY)])
                for d in range(1, NY)
            ]
            totals = jnp.stack(totals)
        if grams is not None:
            values, grams, totals = lax.optimization_barrier((values, grams, totals))
        entries = expand(first, place, blocks, values)
        linked = spread(first, tile_home, turned, swap_parts(entries, NEAR), start.shape[1])
        return linked, totals, grams

    arrived = swap_parts(gather(tile_home, start, tiles, sums, ids), NEAR)
    blocks = arrived[:, BODY + 2, :NZ].astype(jnp.int32)
    linked, _, _ = finish(True, blocks, arrived, None)
    degree = linked[COLS : COLS + 1]
    product = start + COUPLING * (degree * start - linked[:COLS])

    def operate(vector, *grams, last=False):
        linked, totals, grams = finish(
            False,
            blocks,
            swap_parts(gather(tile_home, vector, tiles), NEAR),
            jnp.concatenate(grams, axis=1),
            last,
        )
        return vector + COUPLING * (degree * vector - linked), totals, grams

    mixed = gram(start, product)
    twice, _, grams = operate(
        product, mixed, gram(start, start), mixed, gram(product, product)
    )
    step_0, update_0, _ = steps(grams)
    residual = start - turn_mul(step_0, product)
    direction = residual + turn_mul(update_0, start)
    image = product - turn_mul(step_0, twice)
    product_1 = image + turn_mul(update_0, product)

    twice, totals, grams = operate(
        product_1,
        gram(direction, product_1),
        gram(residual, residual),
        gram(residual, product_1),
        gram(product_1, product_1),
        gram(residual, image),
        gram(image, product_1),
        gram(product_1 + COUPLING * degree * product_1, product_1),
        last=True,
    )
    step_1, update_1, next_gram = steps(grams)
    linked = sum_over(owner_gram(place, totals, weight), "core", "z")
    linked, step_1, update_1, next_gram = lax.optimization_barrier(
        (linked, step_1, update_1, next_gram)
    )
    linked = sum_over(linked, "x")
    answer = turn_mul(step_0, start) + turn_mul(step_1, direction)
    residual = residual - turn_mul(step_1, product_1)
    direction = residual + turn_mul(update_1, direction)
    product_2 = image - turn_mul(step_1, twice) + turn_mul(update_1, product_1)

    step_2 = last_step(grams, linked, step_1, update_1, next_gram)
    answer = answer + turn_mul(step_2, direction)
    residual = residual - turn_mul(step_2, product_2)
    return (answer.T, residual.T)


def solution(mesh):
    fine = Mesh(mesh.devices.reshape(NX, NZ, NC, NY), ALL)
    rows, flat = P(ALL, None), P(ALL)
    return jax.shard_map(
        shards,
        mesh=fine,
        in_specs=(rows, rows, rows, flat, flat, flat, P(("x", "z", "core"))),
        out_specs=(rows, rows),
        check_vma=False,
    )
```

```python
import jax
import jax.numpy as jnp
from jax import lax
from jax.experimental import pallas as pl
from jax.experimental.pallas import tpu as pltpu
from jax.sharding import Mesh, PartitionSpec as P

NX, NZ, NC, NY = 4, 8, 2, 4
TILE = 128
COLS = 64
BLOCKS = 4
TILES = 64
PART = COLS // NY
BODY = NZ * PART
EXTRA = 8
PEERS = NX * NC * NY
COUPLING = 0.0625
ALL = ("x", "z", "core", "rep")
NEAR = ("x", "core", "rep")
SIZES = {"x": NX, "z": NZ, "core": NC, "rep": NY}
VMEM = pl.BlockSpec(memory_space=pltpu.VMEM)
SMEM = pl.BlockSpec(memory_space=pltpu.SMEM)
NT = (((1,), (1,)), ((), ()))
TN = (((0,), (0,)), ((), ()))
PARAMS = pltpu.CompilerParams(vmem_limit_bytes=40 * 1024 * 1024)


def shape(*dims, dtype=jnp.float32):
    return jax.ShapeDtypeStruct(dims, dtype)


def mul(first, second):
    return jnp.dot(first, second, precision=lax.Precision.HIGHEST)


def turn_mul(first, second):
    return lax.dot_general(first, second, TN, precision=lax.Precision.HIGHEST)


def gram(first, second):
    return lax.dot_general(first, second, NT, precision=lax.Precision.HIGHEST)


def swap_parts(value, axes):
    return lax.all_to_all(value, axes, split_axis=0, concat_axis=0, tiled=True)


def swap_cores(value):
    return lax.ppermute(value, "core", [(0, 1), (1, 0)])


def sum_over(value, *axes):
    for axis in axes:
        size, step = SIZES[axis], 1
        while step < size:
            value = value + lax.ppermute(value, axis, [(i, i ^ step) for i in range(size)])
            step *= 2
    return value


def tile_places():
    return [
        (t, (t // (NZ * NC) * NC + t % NC) * NY, t // NC % NZ) for t in range(TILES)
    ]


def pieces(value):
    high = value.astype(jnp.bfloat16)
    return high, (value - high.astype(jnp.float32)).astype(jnp.bfloat16)


def build_kernel(count_ref, acct_ref, attr_ref, tiles_ref, turned_ref, sums_ref):
    rows = lax.broadcasted_iota(jnp.int32, (TILE, TILE), 0)
    lanes = lax.broadcasted_iota(jnp.int32, (TILE, TILE), 1)
    for t in range(TILES):
        used = lanes < count_ref[t]
        account_hot = jnp.where((rows == acct_ref[t : t + 1, :]) & used, 1.0, 0.0)
        attrib_hot = jnp.where(rows == attr_ref[t : t + 1, :], 1.0, 0.0)
        account_hot = account_hot.astype(jnp.bfloat16)
        attrib_hot = attrib_hot.astype(jnp.bfloat16)
        tile = lax.dot_general(
            account_hot, attrib_hot, NT, preferred_element_type=jnp.float32
        )
        turned = lax.dot_general(
            attrib_hot, account_hot, NT, preferred_element_type=jnp.float32
        )
        tiles_ref[t] = tile.astype(jnp.bfloat16)
        turned_ref[t] = turned.astype(jnp.bfloat16)
        sums_ref[t : t + 1, :] = jnp.sum(tile, axis=0, keepdims=True)


def build(counts, accounts, attribs):
    return pl.pallas_call(
        build_kernel,
        out_shape=(
            shape(TILES, TILE, TILE, dtype=jnp.bfloat16),
            shape(TILES, TILE, TILE, dtype=jnp.bfloat16),
            shape(TILES, TILE),
        ),
        in_specs=[SMEM, VMEM, VMEM],
        out_specs=(VMEM, VMEM, VMEM),
        compiler_params=PARAMS,
        name="build_tiles",
    )(counts, accounts, attribs)


def gather_kernel(first, home_ref, vector_ref, tiles_ref, *refs):
    out, split = refs[-2:]
    for part, piece in enumerate(pieces(vector_ref[...])):
        split[part * COLS : (part + 1) * COLS, :] = piece
    if first:
        extra_ref, ids = refs[:2]
        for m in range(PEERS):
            out[m, BODY + 2 :, :] = jnp.broadcast_to(ids[m : m + 1, :], (EXTRA - 2, TILE))
    for t, m, z in tile_places():
        home = home_ref[t]
        block = split[:, pl.ds(pl.multiple_of(home * TILE, TILE), TILE)]
        parts = jnp.dot(block, tiles_ref[t], preferred_element_type=jnp.float32)
        value = parts[:COLS] + parts[COLS:]
        for y in range(NY):
            out[m + y, z * PART : (z + 1) * PART, :] = value[y * PART : (y + 1) * PART]
        if first:
            row = BODY + z % 2
            out[m + z // 2, row : row + 1, :] = extra_ref[t : t + 1, :]


def gather(homes, vector, tiles, *extras):
    return pl.pallas_call(
        lambda *refs: gather_kernel(len(extras) > 0, *refs),
        out_shape=shape(PEERS, BODY + (EXTRA if extras else 0), TILE),
        in_specs=[SMEM] + [VMEM] * (2 + len(extras)),
        out_specs=VMEM,
        scratch_shapes=[pltpu.VMEM((2 * COLS, vector.shape[1]), jnp.bfloat16)],
        compiler_params=PARAMS,
        name="gather_tiles",
    )(homes, vector, tiles, *extras)


def collect_kernel(first, place_ref, blocks_ref, in_ref, out_ref):
    out_ref[...] = jnp.zeros_like(out_ref)
    for m in range(PEERS):
        for z in range(NZ):
            at = pl.ds(pl.multiple_of(blocks_ref[m, z] * PART, PART), PART)
            out_ref[z, at, :] += in_ref[m, z * PART : (z + 1) * PART, :]
    if first:
        for m in range(PEERS):
            for i in range(2):
                z = place_ref[0] * 2 + i
                at = pl.ds(COLS + blocks_ref[m, z], 1)
                out_ref[z, at, :] += in_ref[m, BODY + i : BODY + i + 1, :]


def collect(first, place, blocks, arrived):
    return pl.pallas_call(
        lambda *refs: collect_kernel(first, *refs),
        out_shape=shape(NZ, COLS + (EXTRA if first else 0), TILE),
        in_specs=[SMEM, SMEM, VMEM],
        out_specs=VMEM,
        compiler_params=PARAMS,
        name="collect_blocks",
    )(place, blocks, arrived)


def scale_kernel(first, in_ref, weight_ref, out_ref, sums_ref):
    total = in_ref[0]
    for z in range(1, NZ):
        total = total + in_ref[z]
    weight = weight_ref[...].astype(jnp.float32)
    scaled = [
        total[b * PART : (b + 1) * PART] * weight[b : b + 1] for b in range(BLOCKS)
    ]
    sums_ref[...] = total[:COLS]
    for z in range(NZ):
        for b in range(BLOCKS):
            out_ref[z, b * PART : (b + 1) * PART, :] = scaled[b]
        if first:
            out_ref[z, COLS : COLS + BLOCKS, :] = total[COLS : COLS + BLOCKS] * weight
            out_ref[z, COLS + BLOCKS :, :] = total[COLS + BLOCKS :]


def scale(first, parts, weight):
    return pl.pallas_call(
        lambda *refs: scale_kernel(first, *refs),
        out_shape=(shape(NZ, COLS + (EXTRA if first else 0), TILE), shape(COLS, TILE)),
        in_specs=[VMEM, VMEM],
        out_specs=(VMEM, VMEM),
        compiler_params=PARAMS,
        name="scale_sums",
    )(parts, weight)


def expand_kernel(first, place_ref, blocks_ref, in_ref, out_ref):
    for m in range(PEERS):
        for z in range(NZ):
            at = pl.ds(pl.multiple_of(blocks_ref[m, z] * PART, PART), PART)
            out_ref[m, z * PART : (z + 1) * PART, :] = in_ref[z, at, :]
        if first:
            out_ref[m, BODY:, :] = jnp.zeros((EXTRA, TILE), jnp.float32)
            for i in range(2):
                z = place_ref[0] * 2 + i
                at = pl.ds(COLS + blocks_ref[m, z], 1)
                out_ref[m, BODY + i : BODY + i + 1, :] = in_ref[z, at, :]


def expand(first, place, blocks, values):
    return pl.pallas_call(
        lambda *refs: expand_kernel(first, *refs),
        out_shape=shape(PEERS, BODY + (EXTRA if first else 0), TILE),
        in_specs=[SMEM, SMEM, VMEM],
        out_specs=VMEM,
        compiler_params=PARAMS,
        name="expand_blocks",
    )(place, blocks, values)


def spread_kernel(first, home_ref, turned_ref, in_ref, out_ref):
    out_ref[...] = jnp.zeros_like(out_ref)
    rows = out_ref.shape[0]
    for t, m, z in tile_places():
        at = pl.ds(pl.multiple_of(home_ref[t] * TILE, TILE), TILE)
        values = [in_ref[m + y, z * PART : (z + 1) * PART, :] for y in range(NY)]
        if first:
            row = BODY + z % 2
            count = in_ref[m + z // 2, row : row + 1, :]
            values.append(jnp.broadcast_to(count, (EXTRA, TILE)))
        split = pieces(jnp.concatenate(values, axis=0))
        stack = jnp.concatenate([p.astype(jnp.float32) for p in split], axis=0)
        parts = jnp.dot(
            stack.astype(jnp.bfloat16), turned_ref[t], preferred_element_type=jnp.float32
        )
        out_ref[:, at] += parts[:rows] + parts[rows:]


def spread(first, homes, turned, arrived, accounts):
    rows = COLS + (EXTRA if first else 0)
    return pl.pallas_call(
        lambda *refs: spread_kernel(first, *refs),
        out_shape=shape(rows, accounts),
        in_specs=[SMEM, VMEM, VMEM],
        out_specs=VMEM,
        compiler_params=PARAMS,
        name="spread_tiles",
    )(homes, turned, arrived)


def eliminate(systems):
    rows = lax.broadcasted_iota(jnp.int32, (COLS, 2 * COLS), 0)
    for k in range(COLS):
        after = []
        for system in systems:
            pivot = system[k : k + 1, :] * (1.0 / system[k : k + 1, k : k + 1])
            rest = system - system[:, k : k + 1] * pivot
            after.append(jnp.where(rows == k, pivot, rest))
        systems = after
    return [system[:, COLS:] for system in systems]


def step_kernel(pack_ref, step_ref, update_ref, next_ref):
    res_gram = pack_ref[:, COLS : 2 * COLS]
    mixed, square = pack_ref[:, 2 * COLS : 3 * COLS], pack_ref[:, 3 * COLS : 4 * COLS]
    rows = lax.broadcasted_iota(jnp.int32, (COLS, COLS), 0)
    unit = (rows == lax.broadcasted_iota(jnp.int32, (COLS, COLS), 1)).astype(jnp.float32)
    step, inverse = eliminate(
        [pack_ref[:, : 2 * COLS], jnp.concatenate([res_gram, unit], axis=1)]
    )
    cross = mul(mixed, step)
    next_gram = res_gram - cross - cross.T + turn_mul(step, mul(square, step))
    step_ref[...] = step
    update_ref[...] = mul(inverse, next_gram)
    next_ref[...] = next_gram


def steps(pack):
    return pl.pallas_call(
        step_kernel,
        out_shape=(shape(COLS, COLS),) * 3,
        in_specs=[VMEM],
        out_specs=(VMEM,) * 3,
        compiler_params=PARAMS,
        name="step_matrices",
    )(pack)


def owner_gram_kernel(place_ref, in_ref, weight_ref, out_ref, whole):
    weight = weight_ref[...].astype(jnp.float32)
    for d in range(NY):
        source = lax.rem(place_ref[0] + NY - d, NY)
        at = pl.ds(pl.multiple_of(source * PART, PART), PART)
        for b in range(BLOCKS):
            whole[at, b * TILE : (b + 1) * TILE] = in_ref[d, b * PART : (b + 1) * PART, :]
    scale = jnp.concatenate([weight[b : b + 1] for b in range(BLOCKS)], axis=1)
    out_ref[...] = gram(whole[...] * scale, whole[...])


def owner_gram(place, quarters, weight):
    return pl.pallas_call(
        owner_gram_kernel,
        out_shape=shape(COLS, COLS),
        in_specs=[SMEM, VMEM, VMEM],
        out_specs=VMEM,
        scratch_shapes=[pltpu.VMEM((COLS, BLOCKS * TILE), jnp.float32)],
        compiler_params=PARAMS,
        name="owner_gram",
    )(place, quarters, weight)


def last_kernel(pack_ref, linked_ref, step_ref, update_ref, next_ref, last_ref):
    curvature = pack_ref[:, :COLS]
    mixed, square = pack_ref[:, 2 * COLS : 3 * COLS], pack_ref[:, 3 * COLS : 4 * COLS]
    image_r, image_p = pack_ref[:, 4 * COLS : 5 * COLS], pack_ref[:, 5 * COLS : 6 * COLS]
    step, update = step_ref[...], update_ref[...]
    own = pack_ref[:, 6 * COLS : 7 * COLS] - COUPLING * linked_ref[...]
    half = mul(mixed, update) - mul(image_p, step) - turn_mul(step, mul(square, update))
    whole = image_r + turn_mul(step, mul(own, step))
    whole = whole + turn_mul(update, mul(curvature, update)) + half + half.T
    last_ref[...] = eliminate([jnp.concatenate([whole, next_ref[...]], axis=1)])[0]


def last_step(*matrices):
    return pl.pallas_call(
        last_kernel,
        out_shape=shape(COLS, COLS),
        in_specs=[VMEM] * 5,
        out_specs=VMEM,
        compiler_params=PARAMS,
        name="last_step_matrix",
    )(*matrices)


def shards(
    right_side, tile_account, tile_attribute, tile_count, tile_home, tile_block, attribute_weight
):
    y_at = lax.axis_index("rep")
    place = y_at.reshape(1)
    even = lax.axis_index("core") == 0
    start = right_side.T
    weight = attribute_weight.reshape(BLOCKS, TILE)
    tiles, turned, sums = build(tile_count, tile_account, tile_attribute)
    ids = tile_block.reshape(NX, NZ, NC).transpose(0, 2, 1).reshape(NX * NC, NZ)
    ids = jnp.pad(
        jnp.repeat(ids, NY, axis=0).astype(jnp.float32), ((0, 0), (0, TILE - NZ))
    )

    def finish(first, blocks, arrived, grams, last=False):
        if grams is not None:
            low, high = jnp.split(grams, 2, axis=1)
            grams = jnp.where(even, low, high) + swap_cores(jnp.where(even, high, low))
            grams = sum_over(grams, "z")
            arrived, grams = lax.optimization_barrier((arrived, grams))
            grams = sum_over(grams, "x")
        parts = swap_parts(collect(first, place, blocks, arrived), "z")
        if grams is not None:
            parts, grams = lax.optimization_barrier((parts, grams))
        values, totals = scale(first, parts, weight)
        values = swap_parts(values, "z")
        if last:
            totals = [totals] + [
                lax.ppermute(totals, "rep", [(i, (i + d) % NY) for i in range(NY)])
                for d in range(1, NY)
            ]
            totals = jnp.stack(totals)
            values, totals = lax.optimization_barrier((values, totals))
        if grams is not None:
            grams = sum_over(grams, "rep")
            if not last:
                values, grams = lax.optimization_barrier((values, grams))
            other = swap_cores(grams)
            grams = jnp.concatenate(
                [jnp.where(even, grams, other), jnp.where(even, other, grams)], axis=1
            )
        entries = expand(first, place, blocks, values)
        linked = spread(first, tile_home, turned, swap_parts(entries, NEAR), start.shape[1])
        return linked, totals, grams

    arrived = swap_parts(gather(tile_home, start, tiles, sums, ids), NEAR)
    blocks = arrived[:, BODY + 2, :NZ].astype(jnp.int32)
    linked, _, _ = finish(True, blocks, arrived, None)
    degree = linked[COLS : COLS + 1]
    product = start + COUPLING * (degree * start - linked[:COLS])

    def operate(vector, *grams, last=False):
        linked, totals, grams = finish(
            False,
            blocks,
            swap_parts(gather(tile_home, vector, tiles), NEAR),
            jnp.concatenate(grams, axis=1),
            last,
        )
        return vector + COUPLING * (degree * vector - linked), totals, grams

    mixed = gram(start, product)
    twice, _, grams = operate(
        product, mixed, gram(start, start), mixed, gram(product, product)
    )
    step_0, update_0, _ = steps(grams)
    residual = start - turn_mul(step_0, product)
    direction = residual + turn_mul(update_0, start)
    image = product - turn_mul(step_0, twice)
    product_1 = image + turn_mul(update_0, product)

    twice, totals, grams = operate(
        product_1,
        gram(direction, product_1),
        gram(residual, residual),
        gram(residual, product_1),
        gram(product_1, product_1),
        gram(residual, image),
        gram(image, product_1),
        gram(product_1 + COUPLING * degree * product_1, product_1),
        jnp.zeros((COLS, COLS), jnp.float32),
        last=True,
    )
    step_1, update_1, next_gram = steps(grams)
    linked = sum_over(owner_gram(place, totals, weight), "core", "z")
    linked, step_1, update_1, next_gram = lax.optimization_barrier(
        (linked, step_1, update_1, next_gram)
    )
    linked = sum_over(linked, "x")
    answer = turn_mul(step_0, start) + turn_mul(step_1, direction)
    residual = residual - turn_mul(step_1, product_1)
    direction = residual + turn_mul(update_1, direction)
    product_2 = image - turn_mul(step_1, twice) + turn_mul(update_1, product_1)

    step_2 = last_step(grams, linked, step_1, update_1, next_gram)
    answer = answer + turn_mul(step_2, direction)
    residual = residual - turn_mul(step_2, product_2)
    return (answer.T, residual.T)


def solution(mesh):
    fine = Mesh(mesh.devices.reshape(NX, NZ, NC, NY), ALL)
    rows, flat = P(ALL, None), P(ALL)
    return jax.shard_map(
        shards,
        mesh=fine,
        in_specs=(rows, rows, rows, flat, flat, flat, P(("x", "z", "core"))),
        out_specs=(rows, rows),
        check_vma=False,
    )
```

```python
import jax
import jax.numpy as jnp
from jax import lax
from jax.experimental import pallas as pl
from jax.experimental.pallas import tpu as pltpu
from jax.sharding import Mesh, PartitionSpec as P

NX, NZ, NC, NY = 4, 8, 2, 4
TILE = 128
COLS = 64
BLOCKS = 4
TILES = 64
PART = COLS // NY
BODY = NZ * PART
EXTRA = 8
PEERS = NX * NC * NY
COUPLING = 0.0625
ALL = ("x", "z", "core", "rep")
NEAR = ("x", "core", "rep")
SIZES = {"x": NX, "z": NZ, "core": NC, "rep": NY}
VMEM = pl.BlockSpec(memory_space=pltpu.VMEM)
SMEM = pl.BlockSpec(memory_space=pltpu.SMEM)
NT = (((1,), (1,)), ((), ()))
TN = (((0,), (0,)), ((), ()))
PARAMS = pltpu.CompilerParams(vmem_limit_bytes=40 * 1024 * 1024)


def shape(*dims, dtype=jnp.float32):
    return jax.ShapeDtypeStruct(dims, dtype)


def mul(first, second):
    return jnp.dot(first, second, precision=lax.Precision.HIGHEST)


def turn_mul(first, second):
    return lax.dot_general(first, second, TN, precision=lax.Precision.HIGHEST)


def gram(first, second):
    return lax.dot_general(first, second, NT, precision=lax.Precision.HIGHEST)


def swap_parts(value, axes):
    return lax.all_to_all(value, axes, split_axis=0, concat_axis=0, tiled=True)


def swap_cores(value):
    return lax.ppermute(value, "core", [(0, 1), (1, 0)])


def sum_over(value, *axes):
    for axis in axes:
        size, step = SIZES[axis], 1
        while step < size:
            value = value + lax.ppermute(value, axis, [(i, i ^ step) for i in range(size)])
            step *= 2
    return value


def tile_places():
    return [
        (t, (t // (NZ * NC) * NC + t % NC) * NY, t // NC % NZ) for t in range(TILES)
    ]


def pieces(value):
    high = value.astype(jnp.bfloat16)
    return high, (value - high.astype(jnp.float32)).astype(jnp.bfloat16)


def build_kernel(count_ref, acct_ref, attr_ref, tiles_ref, turned_ref, sums_ref):
    rows = lax.broadcasted_iota(jnp.int32, (TILE, TILE), 0)
    lanes = lax.broadcasted_iota(jnp.int32, (TILE, TILE), 1)
    for t in range(TILES):
        used = lanes < count_ref[t]
        account_hot = jnp.where((rows == acct_ref[t : t + 1, :]) & used, 1.0, 0.0)
        attrib_hot = jnp.where(rows == attr_ref[t : t + 1, :], 1.0, 0.0)
        account_hot = account_hot.astype(jnp.bfloat16)
        attrib_hot = attrib_hot.astype(jnp.bfloat16)
        tile = lax.dot_general(
            account_hot, attrib_hot, NT, preferred_element_type=jnp.float32
        )
        turned = lax.dot_general(
            attrib_hot, account_hot, NT, preferred_element_type=jnp.float32
        )
        tiles_ref[t] = tile.astype(jnp.bfloat16)
        turned_ref[t] = turned.astype(jnp.bfloat16)
        sums_ref[t : t + 1, :] = jnp.sum(tile, axis=0, keepdims=True)


def build(counts, accounts, attribs):
    return pl.pallas_call(
        build_kernel,
        out_shape=(
            shape(TILES, TILE, TILE, dtype=jnp.bfloat16),
            shape(TILES, TILE, TILE, dtype=jnp.bfloat16),
            shape(TILES, TILE),
        ),
        in_specs=[SMEM, VMEM, VMEM],
        out_specs=(VMEM, VMEM, VMEM),
        compiler_params=PARAMS,
        name="build_tiles",
    )(counts, accounts, attribs)


def gather_kernel(first, home_ref, vector_ref, tiles_ref, *refs):
    out, split = refs[-2:]
    for part, piece in enumerate(pieces(vector_ref[...])):
        split[part * COLS : (part + 1) * COLS, :] = piece
    if first:
        extra_ref, ids = refs[:2]
        for m in range(PEERS):
            out[m, BODY + 2 :, :] = jnp.broadcast_to(ids[m : m + 1, :], (EXTRA - 2, TILE))
    for t, m, z in tile_places():
        home = home_ref[t]
        block = split[:, pl.ds(pl.multiple_of(home * TILE, TILE), TILE)]
        parts = jnp.dot(block, tiles_ref[t], preferred_element_type=jnp.float32)
        value = parts[:COLS] + parts[COLS:]
        for y in range(NY):
            out[m + y, z * PART : (z + 1) * PART, :] = value[y * PART : (y + 1) * PART]
        if first:
            row = BODY + z % 2
            out[m + z // 2, row : row + 1, :] = extra_ref[t : t + 1, :]


def gather(homes, vector, tiles, *extras):
    return pl.pallas_call(
        lambda *refs: gather_kernel(len(extras) > 0, *refs),
        out_shape=shape(PEERS, BODY + (EXTRA if extras else 0), TILE),
        in_specs=[SMEM] + [VMEM] * (2 + len(extras)),
        out_specs=VMEM,
        scratch_shapes=[pltpu.VMEM((2 * COLS, vector.shape[1]), jnp.bfloat16)],
        compiler_params=PARAMS,
        name="gather_tiles",
    )(homes, vector, tiles, *extras)


def collect_kernel(first, place_ref, blocks_ref, in_ref, out_ref):
    out_ref[...] = jnp.zeros_like(out_ref)
    for m in range(PEERS):
        for z in range(NZ):
            at = pl.ds(pl.multiple_of(blocks_ref[m, z] * PART, PART), PART)
            out_ref[z, at, :] += in_ref[m, z * PART : (z + 1) * PART, :]
    if first:
        for m in range(PEERS):
            for i in range(2):
                z = place_ref[0] * 2 + i
                at = pl.ds(COLS + blocks_ref[m, z], 1)
                out_ref[z, at, :] += in_ref[m, BODY + i : BODY + i + 1, :]


def collect(first, place, blocks, arrived):
    return pl.pallas_call(
        lambda *refs: collect_kernel(first, *refs),
        out_shape=shape(NZ, COLS + (EXTRA if first else 0), TILE),
        in_specs=[SMEM, SMEM, VMEM],
        out_specs=VMEM,
        compiler_params=PARAMS,
        name="collect_blocks",
    )(place, blocks, arrived)


def scale_kernel(first, in_ref, weight_ref, out_ref, sums_ref):
    total = in_ref[0]
    for z in range(1, NZ):
        total = total + in_ref[z]
    weight = weight_ref[...].astype(jnp.float32)
    scaled = [
        total[b * PART : (b + 1) * PART] * weight[b : b + 1] for b in range(BLOCKS)
    ]
    sums_ref[...] = total[:COLS]
    for z in range(NZ):
        for b in range(BLOCKS):
            out_ref[z, b * PART : (b + 1) * PART, :] = scaled[b]
        if first:
            out_ref[z, COLS : COLS + BLOCKS, :] = total[COLS : COLS + BLOCKS] * weight
            out_ref[z, COLS + BLOCKS :, :] = total[COLS + BLOCKS :]


def scale(first, parts, weight):
    return pl.pallas_call(
        lambda *refs: scale_kernel(first, *refs),
        out_shape=(shape(NZ, COLS + (EXTRA if first else 0), TILE), shape(COLS, TILE)),
        in_specs=[VMEM, VMEM],
        out_specs=(VMEM, VMEM),
        compiler_params=PARAMS,
        name="scale_sums",
    )(parts, weight)


def expand_kernel(first, place_ref, blocks_ref, in_ref, out_ref):
    for m in range(PEERS):
        for z in range(NZ):
            at = pl.ds(pl.multiple_of(blocks_ref[m, z] * PART, PART), PART)
            out_ref[m, z * PART : (z + 1) * PART, :] = in_ref[z, at, :]
        if first:
            out_ref[m, BODY:, :] = jnp.zeros((EXTRA, TILE), jnp.float32)
            for i in range(2):
                z = place_ref[0] * 2 + i
                at = pl.ds(COLS + blocks_ref[m, z], 1)
                out_ref[m, BODY + i : BODY + i + 1, :] = in_ref[z, at, :]


def expand(first, place, blocks, values):
    return pl.pallas_call(
        lambda *refs: expand_kernel(first, *refs),
        out_shape=shape(PEERS, BODY + (EXTRA if first else 0), TILE),
        in_specs=[SMEM, SMEM, VMEM],
        out_specs=VMEM,
        compiler_params=PARAMS,
        name="expand_blocks",
    )(place, blocks, values)


def spread_kernel(first, home_ref, turned_ref, in_ref, out_ref):
    out_ref[...] = jnp.zeros_like(out_ref)
    rows = out_ref.shape[0]
    for t, m, z in tile_places():
        at = pl.ds(pl.multiple_of(home_ref[t] * TILE, TILE), TILE)
        values = [in_ref[m + y, z * PART : (z + 1) * PART, :] for y in range(NY)]
        if first:
            row = BODY + z % 2
            count = in_ref[m + z // 2, row : row + 1, :]
            values.append(jnp.broadcast_to(count, (EXTRA, TILE)))
        split = pieces(jnp.concatenate(values, axis=0))
        stack = jnp.concatenate([p.astype(jnp.float32) for p in split], axis=0)
        parts = jnp.dot(
            stack.astype(jnp.bfloat16), turned_ref[t], preferred_element_type=jnp.float32
        )
        out_ref[:, at] += parts[:rows] + parts[rows:]


def spread(first, homes, turned, arrived, accounts):
    rows = COLS + (EXTRA if first else 0)
    return pl.pallas_call(
        lambda *refs: spread_kernel(first, *refs),
        out_shape=shape(rows, accounts),
        in_specs=[SMEM, VMEM, VMEM],
        out_specs=VMEM,
        compiler_params=PARAMS,
        name="spread_tiles",
    )(homes, turned, arrived)


def eliminate(systems):
    rows = lax.broadcasted_iota(jnp.int32, (COLS, 2 * COLS), 0)
    for k in range(COLS):
        after = []
        for system in systems:
            pivot = system[k : k + 1, :] * (1.0 / system[k : k + 1, k : k + 1])
            rest = system - system[:, k : k + 1] * pivot
            after.append(jnp.where(rows == k, pivot, rest))
        systems = after
    return [system[:, COLS:] for system in systems]


def step_kernel(pack_ref, step_ref, update_ref, next_ref):
    res_gram = pack_ref[:, COLS : 2 * COLS]
    mixed, square = pack_ref[:, 2 * COLS : 3 * COLS], pack_ref[:, 3 * COLS : 4 * COLS]
    rows = lax.broadcasted_iota(jnp.int32, (COLS, COLS), 0)
    unit = (rows == lax.broadcasted_iota(jnp.int32, (COLS, COLS), 1)).astype(jnp.float32)
    step, inverse = eliminate(
        [pack_ref[:, : 2 * COLS], jnp.concatenate([res_gram, unit], axis=1)]
    )
    cross = mul(mixed, step)
    next_gram = res_gram - cross - cross.T + turn_mul(step, mul(square, step))
    step_ref[...] = step
    update_ref[...] = mul(inverse, next_gram)
    next_ref[...] = next_gram


def steps(pack):
    return pl.pallas_call(
        step_kernel,
        out_shape=(shape(COLS, COLS),) * 3,
        in_specs=[VMEM],
        out_specs=(VMEM,) * 3,
        compiler_params=PARAMS,
        name="step_matrices",
    )(pack)


def owner_gram_kernel(place_ref, in_ref, weight_ref, out_ref, whole):
    weight = weight_ref[...].astype(jnp.float32)
    for d in range(NY):
        source = lax.rem(place_ref[0] + NY - d, NY)
        at = pl.ds(pl.multiple_of(source * PART, PART), PART)
        for b in range(BLOCKS):
            whole[at, b * TILE : (b + 1) * TILE] = in_ref[d, b * PART : (b + 1) * PART, :]
    scale = jnp.concatenate([weight[b : b + 1] for b in range(BLOCKS)], axis=1)
    out_ref[...] = gram(whole[...] * scale, whole[...])


def owner_gram(place, quarters, weight):
    return pl.pallas_call(
        owner_gram_kernel,
        out_shape=shape(COLS, COLS),
        in_specs=[SMEM, VMEM, VMEM],
        out_specs=VMEM,
        scratch_shapes=[pltpu.VMEM((COLS, BLOCKS * TILE), jnp.float32)],
        compiler_params=PARAMS,
        name="owner_gram",
    )(place, quarters, weight)


def last_kernel(pack_ref, linked_ref, step_ref, update_ref, next_ref, last_ref):
    curvature = pack_ref[:, :COLS]
    mixed, square = pack_ref[:, 2 * COLS : 3 * COLS], pack_ref[:, 3 * COLS : 4 * COLS]
    image_r, image_p = pack_ref[:, 4 * COLS : 5 * COLS], pack_ref[:, 5 * COLS : 6 * COLS]
    step, update = step_ref[...], update_ref[...]
    own = pack_ref[:, 6 * COLS : 7 * COLS] - COUPLING * linked_ref[...]
    half = mul(mixed, update) - mul(image_p, step) - turn_mul(step, mul(square, update))
    whole = image_r + turn_mul(step, mul(own, step))
    whole = whole + turn_mul(update, mul(curvature, update)) + half + half.T
    last_ref[...] = eliminate([jnp.concatenate([whole, next_ref[...]], axis=1)])[0]


def last_step(*matrices):
    return pl.pallas_call(
        last_kernel,
        out_shape=shape(COLS, COLS),
        in_specs=[VMEM] * 5,
        out_specs=VMEM,
        compiler_params=PARAMS,
        name="last_step_matrix",
    )(*matrices)


def shards(
    right_side, tile_account, tile_attribute, tile_count, tile_home, tile_block, attribute_weight
):
    y_at = lax.axis_index("rep")
    place = y_at.reshape(1)
    even = lax.axis_index("core") == 0
    start = right_side.T
    weight = attribute_weight.reshape(BLOCKS, TILE)
    tiles, turned, sums = build(tile_count, tile_account, tile_attribute)
    ids = tile_block.reshape(NX, NZ, NC).transpose(0, 2, 1).reshape(NX * NC, NZ)
    ids = jnp.pad(
        jnp.repeat(ids, NY, axis=0).astype(jnp.float32), ((0, 0), (0, TILE - NZ))
    )

    def finish(first, blocks, arrived, grams, last=False):
        if grams is not None:
            low, high = jnp.split(grams, 2, axis=1)
            grams = jnp.where(even, low, high) + swap_cores(jnp.where(even, high, low))
            grams = sum_over(grams, "z")
            arrived, grams = lax.optimization_barrier((arrived, grams))
            grams = sum_over(grams, "x")
        parts = swap_parts(collect(first, place, blocks, arrived), "z")
        if grams is not None:
            parts, grams = lax.optimization_barrier((parts, grams))
        values, totals = scale(first, parts, weight)
        values = swap_parts(values, "z")
        if last:
            totals = [totals] + [
                lax.ppermute(totals, "rep", [(i, (i + d) % NY) for i in range(NY)])
                for d in range(1, NY)
            ]
            totals = jnp.stack(totals)
        if grams is not None:
            grams = sum_over(grams, "rep")
            values, grams, totals = lax.optimization_barrier((values, grams, totals))
            other = swap_cores(grams)
            grams = jnp.concatenate(
                [jnp.where(even, grams, other), jnp.where(even, other, grams)], axis=1
            )
        entries = expand(first, place, blocks, values)
        linked = spread(first, tile_home, turned, swap_parts(entries, NEAR), start.shape[1])
        return linked, totals, grams

    arrived = swap_parts(gather(tile_home, start, tiles, sums, ids), NEAR)
    blocks = arrived[:, BODY + 2, :NZ].astype(jnp.int32)
    linked, _, _ = finish(True, blocks, arrived, None)
    degree = linked[COLS : COLS + 1]
    product = start + COUPLING * (degree * start - linked[:COLS])

    def operate(vector, *grams, last=False):
        linked, totals, grams = finish(
            False,
            blocks,
            swap_parts(gather(tile_home, vector, tiles), NEAR),
            jnp.concatenate(grams, axis=1),
            last,
        )
        return vector + COUPLING * (degree * vector - linked), totals, grams

    mixed = gram(start, product)
    twice, _, grams = operate(
        product, mixed, gram(start, start), mixed, gram(product, product)
    )
    step_0, update_0, _ = steps(grams)
    residual = start - turn_mul(step_0, product)
    direction = residual + turn_mul(update_0, start)
    image = product - turn_mul(step_0, twice)
    product_1 = image + turn_mul(update_0, product)

    twice, totals, grams = operate(
        product_1,
        gram(direction, product_1),
        gram(residual, residual),
        gram(residual, product_1),
        gram(product_1, product_1),
        gram(residual, image),
        gram(image, product_1),
        gram(product_1 + COUPLING * degree * product_1, product_1),
        jnp.zeros((COLS, COLS), jnp.float32),
        last=True,
    )
    step_1, update_1, next_gram = steps(grams)
    linked = sum_over(owner_gram(place, totals, weight), "core", "z")
    linked, step_1, update_1, next_gram = lax.optimization_barrier(
        (linked, step_1, update_1, next_gram)
    )
    linked = sum_over(linked, "x")
    answer = turn_mul(step_0, start) + turn_mul(step_1, direction)
    residual = residual - turn_mul(step_1, product_1)
    direction = residual + turn_mul(update_1, direction)
    product_2 = image - turn_mul(step_1, twice) + turn_mul(update_1, product_1)

    step_2 = last_step(grams, linked, step_1, update_1, next_gram)
    answer = answer + turn_mul(step_2, direction)
    residual = residual - turn_mul(step_2, product_2)
    return (answer.T, residual.T)


def solution(mesh):
    fine = Mesh(mesh.devices.reshape(NX, NZ, NC, NY), ALL)
    rows, flat = P(ALL, None), P(ALL)
    return jax.shard_map(
        shards,
        mesh=fine,
        in_specs=(rows, rows, rows, flat, flat, flat, P(("x", "z", "core"))),
        out_specs=(rows, rows),
        check_vma=False,
    )
```

```python
import jax
import jax.numpy as jnp
from jax import lax
from jax.experimental import pallas as pl
from jax.experimental.pallas import tpu as pltpu
from jax.sharding import Mesh, PartitionSpec as P

NX, NZ, NC, NY = 4, 8, 2, 4
TILE = 128
COLS = 64
BLOCKS = 4
TILES = 64
PART = COLS // NY
BODY = NZ * PART
EXTRA = 8
PEERS = NX * NC * NY
COUPLING = 0.0625
ALL = ("x", "z", "core", "rep")
NEAR = ("x", "core", "rep")
SIZES = {"x": NX, "z": NZ, "core": NC, "rep": NY}
VMEM = pl.BlockSpec(memory_space=pltpu.VMEM)
SMEM = pl.BlockSpec(memory_space=pltpu.SMEM)
NT = (((1,), (1,)), ((), ()))
TN = (((0,), (0,)), ((), ()))
PARAMS = pltpu.CompilerParams(vmem_limit_bytes=40 * 1024 * 1024)


def shape(*dims, dtype=jnp.float32):
    return jax.ShapeDtypeStruct(dims, dtype)


def mul(first, second):
    return jnp.dot(first, second, precision=lax.Precision.HIGHEST)


def turn_mul(first, second):
    return lax.dot_general(first, second, TN, precision=lax.Precision.HIGHEST)


def gram(first, second):
    return lax.dot_general(first, second, NT, precision=lax.Precision.HIGHEST)


def swap_parts(value, axes):
    return lax.all_to_all(value, axes, split_axis=0, concat_axis=0, tiled=True)


def swap_cores(value):
    return lax.ppermute(value, "core", [(0, 1), (1, 0)])


def sum_over(value, *axes):
    for axis in axes:
        size, step = SIZES[axis], 1
        while step < size:
            value = value + lax.ppermute(value, axis, [(i, i ^ step) for i in range(size)])
            step *= 2
    return value


def tile_places():
    return [
        (t, (t // (NZ * NC) * NC + t % NC) * NY, t // NC % NZ) for t in range(TILES)
    ]


def pieces(value):
    high = value.astype(jnp.bfloat16)
    return high, (value - high.astype(jnp.float32)).astype(jnp.bfloat16)


def build_kernel(count_ref, acct_ref, attr_ref, tiles_ref, turned_ref, sums_ref):
    rows = lax.broadcasted_iota(jnp.int32, (TILE, TILE), 0)
    lanes = lax.broadcasted_iota(jnp.int32, (TILE, TILE), 1)
    for t in range(TILES):
        used = lanes < count_ref[t]
        account_hot = jnp.where((rows == acct_ref[t : t + 1, :]) & used, 1.0, 0.0)
        attrib_hot = jnp.where(rows == attr_ref[t : t + 1, :], 1.0, 0.0)
        account_hot = account_hot.astype(jnp.bfloat16)
        attrib_hot = attrib_hot.astype(jnp.bfloat16)
        tile = lax.dot_general(
            account_hot, attrib_hot, NT, preferred_element_type=jnp.float32
        )
        turned = lax.dot_general(
            attrib_hot, account_hot, NT, preferred_element_type=jnp.float32
        )
        tiles_ref[t] = tile.astype(jnp.bfloat16)
        turned_ref[t] = turned.astype(jnp.bfloat16)
        sums_ref[t : t + 1, :] = jnp.sum(tile, axis=0, keepdims=True)


def build(counts, accounts, attribs):
    return pl.pallas_call(
        build_kernel,
        out_shape=(
            shape(TILES, TILE, TILE, dtype=jnp.bfloat16),
            shape(TILES, TILE, TILE, dtype=jnp.bfloat16),
            shape(TILES, TILE),
        ),
        in_specs=[SMEM, VMEM, VMEM],
        out_specs=(VMEM, VMEM, VMEM),
        compiler_params=PARAMS,
        name="build_tiles",
    )(counts, accounts, attribs)


def gather_kernel(first, home_ref, vector_ref, tiles_ref, *refs):
    out, split = refs[-2:]
    for part, piece in enumerate(pieces(vector_ref[...])):
        split[part * COLS : (part + 1) * COLS, :] = piece
    if first:
        extra_ref, ids = refs[:2]
        for m in range(PEERS):
            out[m, BODY + 2 :, :] = jnp.broadcast_to(ids[m : m + 1, :], (EXTRA - 2, TILE))
    for t, m, z in tile_places():
        home = home_ref[t]
        block = split[:, pl.ds(pl.multiple_of(home * TILE, TILE), TILE)]
        parts = jnp.dot(block, tiles_ref[t], preferred_element_type=jnp.float32)
        value = parts[:COLS] + parts[COLS:]
        for y in range(NY):
            out[m + y, z * PART : (z + 1) * PART, :] = value[y * PART : (y + 1) * PART]
        if first:
            row = BODY + z % 2
            out[m + z // 2, row : row + 1, :] = extra_ref[t : t + 1, :]


def gather(homes, vector, tiles, *extras):
    return pl.pallas_call(
        lambda *refs: gather_kernel(len(extras) > 0, *refs),
        out_shape=shape(PEERS, BODY + (EXTRA if extras else 0), TILE),
        in_specs=[SMEM] + [VMEM] * (2 + len(extras)),
        out_specs=VMEM,
        scratch_shapes=[pltpu.VMEM((2 * COLS, vector.shape[1]), jnp.bfloat16)],
        compiler_params=PARAMS,
        name="gather_tiles",
    )(homes, vector, tiles, *extras)


def collect_kernel(first, place_ref, blocks_ref, in_ref, out_ref):
    out_ref[...] = jnp.zeros_like(out_ref)
    for m in range(PEERS):
        for z in range(NZ):
            at = pl.ds(pl.multiple_of(blocks_ref[m, z] * PART, PART), PART)
            out_ref[z, at, :] += in_ref[m, z * PART : (z + 1) * PART, :]
    if first:
        for m in range(PEERS):
            for i in range(2):
                z = place_ref[0] * 2 + i
                at = pl.ds(COLS + blocks_ref[m, z], 1)
                out_ref[z, at, :] += in_ref[m, BODY + i : BODY + i + 1, :]


def collect(first, place, blocks, arrived):
    return pl.pallas_call(
        lambda *refs: collect_kernel(first, *refs),
        out_shape=shape(NZ, COLS + (EXTRA if first else 0), TILE),
        in_specs=[SMEM, SMEM, VMEM],
        out_specs=VMEM,
        compiler_params=PARAMS,
        name="collect_blocks",
    )(place, blocks, arrived)


def scale_kernel(first, in_ref, weight_ref, out_ref, sums_ref):
    total = in_ref[0]
    for z in range(1, NZ):
        total = total + in_ref[z]
    weight = weight_ref[...].astype(jnp.float32)
    scaled = [
        total[b * PART : (b + 1) * PART] * weight[b : b + 1] for b in range(BLOCKS)
    ]
    sums_ref[...] = total[:COLS]
    for z in range(NZ):
        for b in range(BLOCKS):
            out_ref[z, b * PART : (b + 1) * PART, :] = scaled[b]
        if first:
            out_ref[z, COLS : COLS + BLOCKS, :] = total[COLS : COLS + BLOCKS] * weight
            out_ref[z, COLS + BLOCKS :, :] = total[COLS + BLOCKS :]


def scale(first, parts, weight):
    return pl.pallas_call(
        lambda *refs: scale_kernel(first, *refs),
        out_shape=(shape(NZ, COLS + (EXTRA if first else 0), TILE), shape(COLS, TILE)),
        in_specs=[VMEM, VMEM],
        out_specs=(VMEM, VMEM),
        compiler_params=PARAMS,
        name="scale_sums",
    )(parts, weight)


def expand_kernel(first, place_ref, blocks_ref, in_ref, out_ref):
    for m in range(PEERS):
        for z in range(NZ):
            at = pl.ds(pl.multiple_of(blocks_ref[m, z] * PART, PART), PART)
            out_ref[m, z * PART : (z + 1) * PART, :] = in_ref[z, at, :]
        if first:
            out_ref[m, BODY:, :] = jnp.zeros((EXTRA, TILE), jnp.float32)
            for i in range(2):
                z = place_ref[0] * 2 + i
                at = pl.ds(COLS + blocks_ref[m, z], 1)
                out_ref[m, BODY + i : BODY + i + 1, :] = in_ref[z, at, :]


def expand(first, place, blocks, values):
    return pl.pallas_call(
        lambda *refs: expand_kernel(first, *refs),
        out_shape=shape(PEERS, BODY + (EXTRA if first else 0), TILE),
        in_specs=[SMEM, SMEM, VMEM],
        out_specs=VMEM,
        compiler_params=PARAMS,
        name="expand_blocks",
    )(place, blocks, values)


def spread_kernel(first, home_ref, turned_ref, in_ref, out_ref):
    out_ref[...] = jnp.zeros_like(out_ref)
    rows = out_ref.shape[0]
    for t, m, z in tile_places():
        at = pl.ds(pl.multiple_of(home_ref[t] * TILE, TILE), TILE)
        values = [in_ref[m + y, z * PART : (z + 1) * PART, :] for y in range(NY)]
        if first:
            row = BODY + z % 2
            count = in_ref[m + z // 2, row : row + 1, :]
            values.append(jnp.broadcast_to(count, (EXTRA, TILE)))
        split = pieces(jnp.concatenate(values, axis=0))
        stack = jnp.concatenate([p.astype(jnp.float32) for p in split], axis=0)
        parts = jnp.dot(
            stack.astype(jnp.bfloat16), turned_ref[t], preferred_element_type=jnp.float32
        )
        out_ref[:, at] += parts[:rows] + parts[rows:]


def spread(first, homes, turned, arrived, accounts):
    rows = COLS + (EXTRA if first else 0)
    return pl.pallas_call(
        lambda *refs: spread_kernel(first, *refs),
        out_shape=shape(rows, accounts),
        in_specs=[SMEM, VMEM, VMEM],
        out_specs=VMEM,
        compiler_params=PARAMS,
        name="spread_tiles",
    )(homes, turned, arrived)


def eliminate(systems):
    rows = lax.broadcasted_iota(jnp.int32, (COLS, 2 * COLS), 0)
    for k in range(COLS):
        after = []
        for system in systems:
            pivot = system[k : k + 1, :] * (1.0 / system[k : k + 1, k : k + 1])
            rest = system - system[:, k : k + 1] * pivot
            after.append(jnp.where(rows == k, pivot, rest))
        systems = after
    return [system[:, COLS:] for system in systems]


def step_kernel(pack_ref, step_ref, update_ref, next_ref):
    res_gram = pack_ref[:, COLS : 2 * COLS]
    mixed, square = pack_ref[:, 2 * COLS : 3 * COLS], pack_ref[:, 3 * COLS : 4 * COLS]
    rows = lax.broadcasted_iota(jnp.int32, (COLS, COLS), 0)
    unit = (rows == lax.broadcasted_iota(jnp.int32, (COLS, COLS), 1)).astype(jnp.float32)
    step, inverse = eliminate(
        [pack_ref[:, : 2 * COLS], jnp.concatenate([res_gram, unit], axis=1)]
    )
    cross = mul(mixed, step)
    next_gram = res_gram - cross - cross.T + turn_mul(step, mul(square, step))
    step_ref[...] = step
    update_ref[...] = mul(inverse, next_gram)
    next_ref[...] = next_gram


def steps(pack):
    return pl.pallas_call(
        step_kernel,
        out_shape=(shape(COLS, COLS),) * 3,
        in_specs=[VMEM],
        out_specs=(VMEM,) * 3,
        compiler_params=PARAMS,
        name="step_matrices",
    )(pack)


def owner_gram_kernel(place_ref, in_ref, weight_ref, out_ref, whole):
    weight = weight_ref[...].astype(jnp.float32)
    for d in range(NY):
        source = lax.rem(place_ref[0] + NY - d, NY)
        at = pl.ds(pl.multiple_of(source * PART, PART), PART)
        for b in range(BLOCKS):
            whole[at, b * TILE : (b + 1) * TILE] = in_ref[d, b * PART : (b + 1) * PART, :]
    scale = jnp.concatenate([weight[b : b + 1] for b in range(BLOCKS)], axis=1)
    out_ref[...] = gram(whole[...] * scale, whole[...])


def owner_gram(place, quarters, weight):
    return pl.pallas_call(
        owner_gram_kernel,
        out_shape=shape(COLS, COLS),
        in_specs=[SMEM, VMEM, VMEM],
        out_specs=VMEM,
        scratch_shapes=[pltpu.VMEM((COLS, BLOCKS * TILE), jnp.float32)],
        compiler_params=PARAMS,
        name="owner_gram",
    )(place, quarters, weight)


def last_kernel(pack_ref, linked_ref, step_ref, update_ref, next_ref, last_ref):
    curvature = pack_ref[:, :COLS]
    mixed, square = pack_ref[:, 2 * COLS : 3 * COLS], pack_ref[:, 3 * COLS : 4 * COLS]
    image_r, image_p = pack_ref[:, 4 * COLS : 5 * COLS], pack_ref[:, 5 * COLS : 6 * COLS]
    step, update = step_ref[...], update_ref[...]
    own = pack_ref[:, 6 * COLS : 7 * COLS] - COUPLING * linked_ref[...]
    half = mul(mixed, update) - mul(image_p, step) - turn_mul(step, mul(square, update))
    whole = image_r + turn_mul(step, mul(own, step))
    whole = whole + turn_mul(update, mul(curvature, update)) + half + half.T
    last_ref[...] = eliminate([jnp.concatenate([whole, next_ref[...]], axis=1)])[0]


def last_step(*matrices):
    return pl.pallas_call(
        last_kernel,
        out_shape=shape(COLS, COLS),
        in_specs=[VMEM] * 5,
        out_specs=VMEM,
        compiler_params=PARAMS,
        name="last_step_matrix",
    )(*matrices)


def shards(
    right_side, tile_account, tile_attribute, tile_count, tile_home, tile_block, attribute_weight
):
    y_at = lax.axis_index("rep")
    place = y_at.reshape(1)
    even = lax.axis_index("core") == 0
    start = right_side.T
    weight = attribute_weight.reshape(BLOCKS, TILE)
    tiles, turned, sums = build(tile_count, tile_account, tile_attribute)
    ids = tile_block.reshape(NX, NZ, NC).transpose(0, 2, 1).reshape(NX * NC, NZ)
    ids = jnp.pad(
        jnp.repeat(ids, NY, axis=0).astype(jnp.float32), ((0, 0), (0, TILE - NZ))
    )

    def finish(first, blocks, arrived, grams, last=False):
        if grams is not None:
            low, high = jnp.split(grams, 2, axis=1)
            grams = jnp.where(even, low, high) + swap_cores(jnp.where(even, high, low))
            grams = sum_over(grams, "z")
            arrived, grams = lax.optimization_barrier((arrived, grams))
            grams = sum_over(grams, "x")
        parts = swap_parts(collect(first, place, blocks, arrived), "z")
        if grams is not None:
            parts, grams = lax.optimization_barrier((parts, grams))
        values, totals = scale(first, parts, weight)
        values = swap_parts(values, "z")
        if last:
            totals = [totals] + [
                lax.ppermute(totals, "rep", [(i, (i + d) % NY) for i in range(NY)])
                for d in range(1, NY)
            ]
            totals = sum_over(owner_gram(place, jnp.stack(totals), weight), "core")
        if grams is not None:
            grams = sum_over(grams, "rep")
            values, grams, totals = lax.optimization_barrier((values, grams, totals))
            other = swap_cores(grams)
            grams = jnp.concatenate(
                [jnp.where(even, grams, other), jnp.where(even, other, grams)], axis=1
            )
        entries = expand(first, place, blocks, values)
        linked = spread(first, tile_home, turned, swap_parts(entries, NEAR), start.shape[1])
        return linked, totals, grams

    arrived = swap_parts(gather(tile_home, start, tiles, sums, ids), NEAR)
    blocks = arrived[:, BODY + 2, :NZ].astype(jnp.int32)
    linked, _, _ = finish(True, blocks, arrived, None)
    degree = linked[COLS : COLS + 1]
    product = start + COUPLING * (degree * start - linked[:COLS])

    def operate(vector, *grams, last=False):
        linked, totals, grams = finish(
            False,
            blocks,
            swap_parts(gather(tile_home, vector, tiles), NEAR),
            jnp.concatenate(grams, axis=1),
            last,
        )
        return vector + COUPLING * (degree * vector - linked), totals, grams

    mixed = gram(start, product)
    twice, _, grams = operate(
        product, mixed, gram(start, start), mixed, gram(product, product)
    )
    step_0, update_0, _ = steps(grams)
    residual = start - turn_mul(step_0, product)
    direction = residual + turn_mul(update_0, start)
    product_1 = product + turn_mul(update_0, product)
    moved = turn_mul(step_0, twice)
    product_1 = product_1 - moved
    image = product - moved

    twice, totals, grams = operate(
        product_1,
        gram(direction, product_1),
        gram(residual, residual),
        gram(residual, product_1),
        gram(product_1, product_1),
        gram(residual, image),
        gram(image, product_1),
        gram(product_1 + COUPLING * degree * product_1, product_1),
        jnp.zeros((COLS, COLS), jnp.float32),
        last=True,
    )
    step_1, update_1, next_gram = steps(grams)
    linked = sum_over(totals, "z")
    linked, step_1, update_1, next_gram = lax.optimization_barrier(
        (linked, step_1, update_1, next_gram)
    )
    linked = sum_over(linked, "x")
    answer = turn_mul(step_0, start) + turn_mul(step_1, direction)
    residual = residual - turn_mul(step_1, product_1)
    direction = residual + turn_mul(update_1, direction)
    product_2 = (image + turn_mul(update_1, product_1)) - turn_mul(step_1, twice)

    step_2 = last_step(grams, linked, step_1, update_1, next_gram)
    answer = answer + turn_mul(step_2, direction)
    residual = residual - turn_mul(step_2, product_2)
    return (answer.T, residual.T)


def solution(mesh):
    fine = Mesh(mesh.devices.reshape(NX, NZ, NC, NY), ALL)
    rows, flat = P(ALL, None), P(ALL)
    return jax.shard_map(
        shards,
        mesh=fine,
        in_specs=(rows, rows, rows, flat, flat, flat, P(("x", "z", "core"))),
        out_specs=(rows, rows),
        check_vma=False,
    )
```
